32 devices in a mesh: ctx: 16 (over z, x, core), head: 2 (over y).
Axes of the slice: x: 2, y: 2, z: 4, core: 2. Of those that a mesh axis runs over, the one named last changes fastest.
Arguments:
- mixer_input: bfloat16 [8192, 4096], P('ctx', 'head'), may hold values from -61 to 61
- gate_input: bfloat16 [8192, 4096], P('ctx', 'head'), may hold values from -7.5 to 7.5
- write_vecs: bfloat16 [8192, 128], P('ctx'), may hold values from -0.8984375 to 0.8984375
- read_vecs: bfloat16 [8192, 128], P('ctx'), may hold values from -0.8984375 to 0.8984375
- log_decay: float32 [64, 8192], P('head', 'ctx'), may hold values from -0.76 to 0
- doc_start: int32 [8192], P('ctx'), may hold values from 0 to 1, as said below
- live_mask: int32 [8192], P('ctx'), may hold values from 0 to 1, as said below
- skip_gain: float32 [64], P('head'), may hold values from 0.5 to 2
- norm_gain: float32 [4096], P('head'), may hold values from 0.25 to 1.75
- residual: bfloat16 [8192, 2048], P('ctx', 'head'), may hold values from -61 to 61
- out_weight: bfloat16 [4096, 2048], P(('head', 'ctx')), may hold values from -0.09375 to 0.09375
- mlp_gain: float32 [2048], replicated, may hold values from 0.25 to 1.75
- gate_weight: bfloat16 [2048, 4096], P('ctx', 'head'), may hold values from -0.125 to 0.125
- up_weight: bfloat16 [2048, 4096], P('ctx', 'head'), may hold values from -0.125 to 0.125
- down_weight: bfloat16 [4096, 2048], P(('head', 'ctx')), may hold values from -0.09375 to 0.09375
Outputs:
- mixed: bfloat16 [8192, 2048], P('ctx', 'head')
The draws below stay inside these ranges and needn't reach their ends.
Inputs may be any that keep to these rules, and one draw needn't show every extreme that they name: `doc_start`: documents begin only at the first token of a group of 256; the window's first token begins one; a document spans at most 16 groups, and some document spans exactly that many. `live_mask`: the 0 entries are the tokens after a document's last real token, all within its last group; every document has a real token.
All inputs are finite; a program needn't handle non-finite values.
Results may differ from the reference program's by a relative error of at most 0.007.
Values may be sent and summed in bfloat16 or wider, within the bound.
A program may use at most 128 MiB of HBM per device.

```python
import math
import jax
import jax.numpy as jnp
from jax import lax

D = 2048
SSM_CHANNEL_NUM = 64
HDIM = 64
STATE = 128
FF = 4096
GROUP = 256
DOC_GROUPS = 16
TOK_DEV = 512
CONTEXT_POSITION = 8192
INNER = 4096
N_CTX = 16


def doc_layout(key):
    group_count = CONTEXT_POSITION // GROUP
    key_lengths = jax.random.fold_in(key, 101)
    key_pick = jax.random.fold_in(key, 102)
    key_padding = jax.random.fold_in(key, 103)
    lengths = jax.random.randint(key_lengths, (group_count,), 1, DOC_GROUPS + 1)
    longest = jax.random.randint(key_pick, (), 0, max(1, group_count // DOC_GROUPS - 1))
    lengths = jnp.where(jnp.arange(group_count) == longest, DOC_GROUPS, lengths).astype(jnp.int32)
    ends = jnp.cumsum(lengths).astype(jnp.int32)
    begins = ends - lengths
    first_group = jnp.zeros((group_count,), jnp.int32).at[begins].set(1, mode='drop')
    closing = jnp.concatenate([first_group[1:], jnp.ones((1,), jnp.int32)])
    padding = jax.random.randint(key_padding, (group_count,), 0, GROUP)
    offsets = jnp.arange(GROUP, dtype=jnp.int32)
    starts = first_group[:, None] * (offsets[None, :] == 0).astype(jnp.int32)
    real_tokens = jnp.where(closing[:, None] == 1, (offsets[None, :] < GROUP - padding[:, None]).astype(jnp.int32), 1)
    return (starts.reshape(-1).astype(jnp.int32), real_tokens.reshape(-1).astype(jnp.int32))


def scaled_field(key, row_count, col_count):
    key_rows = jax.random.fold_in(key, 201)
    key_cols = jax.random.fold_in(key, 202)
    key_noise = jax.random.fold_in(key, 203)
    row_scale = jnp.exp(jax.random.uniform(key_rows, (row_count, 1), jnp.float32, math.log(0.3), math.log(3.0)))
    ramp = 0.6 * jnp.power(3.0, jnp.arange(col_count, dtype=jnp.float32) / col_count)
    col_scale = ramp[None, :] * jnp.exp(jax.random.uniform(key_cols, (1, col_count), jnp.float32, math.log(0.5), math.log(2.0)))
    noise = jnp.clip(jax.random.normal(key_noise, (row_count, col_count), jnp.float32), -4.0, 4.0)
    return noise * row_scale * col_scale


def draw_mixer_input(key, part):
    return scaled_field(key, CONTEXT_POSITION, INNER).astype(jnp.bfloat16)


def draw_residual(key, part):
    return scaled_field(key, CONTEXT_POSITION, D).astype(jnp.bfloat16)


def draw_doc_start(key, part):
    return doc_layout(key)[0]


def draw_live_mask(key, part):
    return doc_layout(key)[1]


def draw_log_decay(key, part):
    sequence_span = DOC_GROUPS * GROUP
    fast_share = 0.5
    key_kind = jax.random.fold_in(key, 301)
    key_fast = jax.random.fold_in(key, 302)
    key_slow = jax.random.fold_in(key, 303)
    key_jitter = jax.random.fold_in(key, 304)
    spike_seed = jax.random.fold_in(key, 305)
    key_depth = jax.random.fold_in(key, 306)
    is_fast = jax.random.uniform(key_kind, (SSM_CHANNEL_NUM, 1), jnp.float32) < fast_share
    fast_rate = jnp.exp(jax.random.uniform(key_fast, (SSM_CHANNEL_NUM, 1), jnp.float32, math.log(1.0 / 50.0), math.log(1.0 / 30.0)))
    slow_rate = jnp.exp(jax.random.uniform(key_slow, (SSM_CHANNEL_NUM, 1), jnp.float32, math.log(0.1), 0.0)) / sequence_span
    ground_frequency = jnp.where(is_fast, fast_rate, slow_rate)
    jitter_perturbation = jnp.exp(jax.random.uniform(key_jitter, (SSM_CHANNEL_NUM, CONTEXT_POSITION), jnp.float32, math.log(0.5), math.log(2.0)))
    spike_occurrences = (jax.random.uniform(spike_seed, (SSM_CHANNEL_NUM, CONTEXT_POSITION), jnp.float32) < 3.0 / sequence_span).astype(jnp.float32)
    level_ordinal = jax.random.uniform(key_depth, (SSM_CHANNEL_NUM, CONTEXT_POSITION), jnp.float32, 0.22, 0.69)
    return -(ground_frequency * jitter_perturbation + spike_occurrences * level_ordinal)


def shard_levels(own_key, dims, split, low, top_value):
    loudness = 1.0
    for dim, shards_of in split:
        steps = jax.random.uniform(jax.random.fold_in(jax.random.fold_in(own_key, 6), dim), (shards_of,), jnp.float32, low / len(split), top_value / len(split))
        loudness = loudness * jnp.repeat(jnp.exp(steps), dims[dim] // shards_of).reshape((-1,) + (1,) * (len(dims) - 1 - dim))
    return loudness


def centred(own_key, shape, spread, reach, cuts=(), kind=jnp.bfloat16):
    level = shard_levels(own_key, shape, cuts, -0.22, 0.18) if cuts else 1.0
    array = jax.random.normal(own_key, shape, jnp.float32) * spread * level
    return jnp.minimum(jnp.maximum(array, -reach), reach).astype(kind)


def setup_inputs(seed: int = 0) -> dict:
    key_list = jax.random.split(jax.random.key(seed), 16)
    return {
        "mixer_input": draw_mixer_input(jax.random.fold_in(key_list[15], 71), 0),
        "gate_input": centred(key_list[1], (CONTEXT_POSITION, INNER), 1.5, 7.5, ((0, 16), (1, 2))),
        "write_vecs": centred(key_list[2], (CONTEXT_POSITION, STATE), 0.15, 0.8984375, ((0, 16),)),
        "read_vecs": centred(key_list[3], (CONTEXT_POSITION, STATE), 0.15, 0.8984375, ((0, 16),)),
        "log_decay": draw_log_decay(jax.random.fold_in(key_list[15], 71), 0),
        "doc_start": draw_doc_start(jax.random.fold_in(key_list[15], 71), 0),
        "live_mask": draw_live_mask(jax.random.fold_in(key_list[15], 71), 0),
        "skip_gain": jnp.clip(jnp.exp(math.log(2.0) - 1.3862944 * jax.random.uniform(key_list[7], (SSM_CHANNEL_NUM,), jnp.float32) ** shard_levels(key_list[7], (SSM_CHANNEL_NUM,), ((0, 2),), -0.2, 0.2)), 0.5, 2.0),
        "norm_gain": jnp.clip(1.0 + 0.15 * jax.random.normal(key_list[8], (INNER,), jnp.float32), 0.25, 1.75),
        "residual": draw_residual(jax.random.fold_in(key_list[15], 71), 0),
        "out_weight": centred(key_list[10], (INNER, D), INNER ** -0.5, 0.09375, ((0, 32),)),
        "mlp_gain": jnp.clip(1.0 + 0.15 * jax.random.normal(key_list[11], (D,), jnp.float32), 0.25, 1.75),
        "gate_weight": centred(key_list[12], (D, FF), D ** -0.5, 0.125, ((0, 16), (1, 2))),
        "up_weight": centred(key_list[13], (D, FF), D ** -0.5, 0.125, ((0, 16), (1, 2))),
        "down_weight": centred(key_list[14], (FF, D), FF ** -0.5, 0.09375, ((0, 32),)),
    }


EPS = 1e-05

def group_core(masked, write_group, read_group, log_group, start_group, skip_gain):
    positions = jnp.arange(GROUP)
    log_sums = jnp.cumsum(log_group, axis=1)
    doc_index = jnp.cumsum(start_group)
    same_doc = (doc_index[:, None] == doc_index[None, :]) & (positions[:, None] >= positions[None, :])
    scores = jnp.dot(read_group, write_group.T, preferred_element_type=jnp.float32)
    log_gaps = jnp.where(same_doc[None], log_sums[:, :, None] - log_sums[:, None, :], 0.0)
    weights = jnp.where(same_doc[None], scores[None] * jnp.exp(log_gaps), 0.0).astype(jnp.bfloat16)
    per_head = masked.reshape(GROUP, -1, HDIM)
    intra_out = jnp.einsum('hij,jhp->ihp', weights.astype(jnp.float32), per_head.astype(jnp.float32))
    tail_wts = jnp.exp(log_sums[:, -1:] - log_sums) * (doc_index == doc_index[-1]).astype(jnp.float32)[None]
    weighted = (write_group.astype(jnp.float32)[None] * tail_wts[:, :, None]).astype(jnp.bfloat16)
    local_state = jnp.einsum('hjn,jhp->hnp', weighted.astype(jnp.float32), per_head.astype(jnp.float32))
    reach_wts = jnp.exp(log_sums) * (doc_index == 0).astype(jnp.float32)[None]
    decay_all = jnp.exp(log_sums[:, -1]) * (doc_index[-1] == 0).astype(jnp.float32)
    direct = intra_out + skip_gain[None, :, None] * per_head.astype(jnp.float32)
    return (direct, local_state, reach_wts, decay_all)

def reference(mixer_input, gate_input, write_vecs, read_vecs, log_decay, doc_start, live_mask, skip_gain, norm_gain, residual, out_weight, mlp_gain, gate_weight, up_weight, down_weight):
    group_count = CONTEXT_POSITION // GROUP
    masked = mixer_input * live_mask.astype(jnp.bfloat16)[:, None]
    group_data = (masked.reshape(group_count, GROUP, INNER), gate_input.reshape(group_count, GROUP, INNER), write_vecs.reshape(group_count, GROUP, STATE), read_vecs.reshape(group_count, GROUP, STATE), log_decay.reshape(SSM_CHANNEL_NUM, group_count, GROUP).transpose(1, 0, 2), doc_start.reshape(group_count, GROUP))

    def advance(carried, pieces):
        x_group, z_group, write_group, read_group, log_group, start_group = pieces
        direct, local_state, reach_wts, decay_all = group_core(x_group, write_group, read_group, log_group, start_group, skip_gain)
        inner_state = carried.astype(jnp.bfloat16)
        crossed = jnp.einsum('in,hnp->ihp', read_group.astype(jnp.float32), inner_state.astype(jnp.float32)) * reach_wts.T[:, :, None]
        output = (direct + crossed).reshape(GROUP, INNER)
        gated = output * jax.nn.silu(z_group.astype(jnp.float32))
        normed = (gated * lax.rsqrt(lax.optimization_barrier(jnp.mean(gated * gated, axis=1, keepdims=True)) + EPS) * norm_gain).astype(jnp.bfloat16)
        return (decay_all[:, None, None] * carried + local_state, normed)
    initial = jnp.zeros((SSM_CHANNEL_NUM, STATE, HDIM), jnp.float32)
    unused, normed = lax.scan(advance, initial, group_data)

    def mlp_block(block_data):
        normed_rows, resid_rows, live_rows = block_data
        hidden = (resid_rows.astype(jnp.float32) + jnp.dot(normed_rows, out_weight, preferred_element_type=jnp.float32)).astype(jnp.bfloat16)
        hidden_f = hidden.astype(jnp.float32)
        scaled = (hidden_f * lax.rsqrt(lax.optimization_barrier(jnp.mean(hidden_f * hidden_f, axis=1, keepdims=True)) + EPS) * mlp_gain).astype(jnp.bfloat16)
        gate_out = jnp.dot(scaled, gate_weight, preferred_element_type=jnp.float32)
        up_out = jnp.dot(scaled, up_weight, preferred_element_type=jnp.float32)
        act = (jax.nn.silu(gate_out) * up_out).astype(jnp.bfloat16)
        down_out = jnp.dot(act, down_weight, preferred_element_type=jnp.float32)
        return (live_rows.astype(jnp.float32)[:, None] * (hidden_f + down_out)).astype(jnp.bfloat16)
    blocks = (normed.reshape(N_CTX, TOK_DEV, INNER), residual.reshape(N_CTX, TOK_DEV, D), live_mask.reshape(N_CTX, TOK_DEV))
    mixed = lax.map(mlp_block, blocks)
    return mixed.reshape(CONTEXT_POSITION, D)
```

```python
import functools

import jax
import jax.numpy as jnp
from jax import lax
from jax.experimental import pallas as pl
from jax.experimental.pallas import tpu as pltpu
from jax.sharding import PartitionSpec as P

HDIM = 64
STATE = 128
GROUP = 256
INNER = 4096
TILE = 256
LANES = 128

EPS = 1e-05
MESH = pl.DeviceIdType.MESH


def carried_in(factor, state):
    n = lax.axis_size("ctx")
    place = lax.axis_index("ctx")
    heads = state.shape[0]
    rows = heads * HDIM // n
    blocks = state.astype(jnp.bfloat16).reshape(n, rows, STATE)
    coarse = factor.astype(jnp.bfloat16)
    fine = (factor - coarse.astype(jnp.float32)).astype(jnp.bfloat16)
    tail = jnp.pad(jnp.stack([coarse, fine]), ((0, 14), (0, LANES - heads)))
    packed = jnp.concatenate([blocks, jnp.broadcast_to(tail[None], (n, 16, LANES))], axis=1)
    packed = lax.all_to_all(packed, "ctx", 0, 0)
    factors = packed[:, rows, :heads].astype(jnp.float32) + packed[:, rows + 1, :heads].astype(
        jnp.float32
    )
    owner = (place * rows + jnp.arange(rows)) // HDIM
    row_factors = jnp.take(factors, owner, axis=1)
    run = jnp.zeros((rows, STATE), jnp.float32)
    entering = []
    for source in range(n):
        entering.append(run.astype(jnp.bfloat16))
        run = row_factors[source][:, None] * run + packed[source, :rows].astype(jnp.float32)
    back = lax.all_to_all(jnp.stack(entering), "ctx", 0, 0)
    return back.reshape(heads, HDIM, STATE).astype(jnp.float32)


def group_core(masked, write_group, read_group, log_group, start_group, skip_gain):
    positions = jnp.arange(GROUP)
    log_sums = jnp.cumsum(log_group, axis=1)
    doc_index = jnp.cumsum(start_group)
    same_doc = (doc_index[:, None] == doc_index[None, :]) & (
        positions[:, None] >= positions[None, :]
    )
    scores = jnp.dot(read_group, write_group.T, preferred_element_type=jnp.float32)
    log_gaps = jnp.where(same_doc[None], log_sums[:, :, None] - log_sums[:, None, :], 0.0)
    weights = jnp.where(same_doc[None], scores[None] * jnp.exp(log_gaps), 0.0).astype(jnp.bfloat16)
    per_head = masked.reshape(GROUP, -1, HDIM)
    intra_out = jnp.einsum("hij,jhp->ihp", weights, per_head, preferred_element_type=jnp.float32)
    tail_wts = (
        jnp.exp(log_sums[:, -1:] - log_sums)
        * (doc_index == doc_index[-1]).astype(jnp.float32)[None]
    )
    weighted = (write_group.astype(jnp.float32)[None] * tail_wts[:, :, None]).astype(jnp.bfloat16)
    local_state = jnp.einsum("hjn,jhp->hpn", weighted, per_head, preferred_element_type=jnp.float32)
    reach_wts = jnp.exp(log_sums) * (doc_index == 0).astype(jnp.float32)[None]
    decay_all = jnp.exp(log_sums[:, -1]) * (doc_index[-1] == 0).astype(jnp.float32)
    direct = intra_out + skip_gain[None, :, None] * per_head.astype(jnp.float32)
    return (direct, local_state, reach_wts, decay_all)


def block_kernel(
    n, peers, normed, res, wout, g_sh, u_sh, d_sh, gain, live, out,
    wg, wu, wd, psend, precv, own, hid, scaled, act, dsend, drecv,
    ring_s, ring_r, x_s, x_r, sib_s, sib_r, y_s, y_r,
):
    me, y = lax.axis_index("ctx"), lax.axis_index("head")
    c, b, a = me % 2, (me // 2) % 2, me // 4
    ring = n // 4
    half = res.shape[1]
    toks = res.shape[0]
    sib = (me + 1 - 2 * c, y)
    across = (me + 2 - 4 * b, y)
    after = (((a + 1) % ring) * 4 + b * 2 + c, y)
    before = (((a + ring - 1) % ring) * 4 + b * 2 + c, y)
    others = [lax.rem(y + j, peers) for j in range(1, peers)]
    mine = pl.multiple_of(y * half, half)
    starts = [pl.multiple_of(other * half, half) for other in others] + [mine]

    barrier = pltpu.get_barrier_semaphore()
    for device in [sib, across, after, before] + [(me, other) for other in others]:
        pl.semaphore_signal(barrier, inc=1, device_id=device, device_id_type=MESH)
    pl.semaphore_wait(barrier, 3 + peers)

    full = [wg, wu] + [wd.at[j] for j in range(peers)]
    shard = [g_sh, u_sh] + [d_sh.at[:, pl.ds(start, half)] for start in starts]
    parts = len(full)

    def rows(p, k, bb, cc):
        slot = ((a + ring - k) % ring) * 4 + bb * 2 + cc
        depth = shard[p].shape[0]
        return pl.ds(pl.multiple_of(slot * depth, depth), depth)

    def remote(src, dst, send, recv, device):
        return pltpu.make_async_remote_copy(
            src_ref=src, dst_ref=dst, send_sem=send, recv_sem=recv,
            device_id=device, device_id_type=MESH,
        )

    def column(p, k):
        place = full[p].at[rows(p, k, b, c)]
        return (shard[p] if k == 0 else place), place

    def ring_copy(p, k):
        src, dst = column(p, k)
        return remote(src, dst, ring_s.at[p, k], ring_r.at[p, k], after)

    def x_copy(p, k):
        src, dst = column(p, k)
        return remote(src, dst, x_s.at[p, k], x_r.at[p, k], across)

    def sib_copy(p, k):
        if k < ring:
            src, dst = column(p, k)
        else:
            src = dst = full[p].at[rows(p, k - ring, 1 - b, c)]
        return remote(src, dst, sib_s.at[p, k], sib_r.at[p, k], sib)

    def spread(p, k):
        if k < ring - 1:
            ring_copy(p, k).start()
        x_copy(p, k).start()
        sib_copy(p, k).start()

    def begin(p):
        spread(p, 0)
        full[p][rows(p, 0, b, c), :] = shard[p][...]

    def ring_step(p, k):
        place = full[p].at[rows(p, k, b, c)]
        remote(place, place, ring_s.at[p, k - 1], ring_r.at[p, k - 1], after).wait_recv()
        spread(p, k)

    def ring_steps(p):
        for k in range(1, ring):
            ring_step(p, k)

    def x_steps(p):
        for k in range(ring):
            place = full[p].at[rows(p, k, 1 - b, c)]
            remote(place, place, x_s.at[p, k], x_r.at[p, k], across).wait_recv()
            sib_copy(p, ring + k).start()

    def finish(p):
        for k in range(2 * ring):
            bb = b if k < ring else 1 - b
            place = full[p].at[rows(p, k % ring, bb, 1 - c)]
            remote(place, place, sib_s.at[p, k], sib_r.at[p, k], sib).wait_recv()

    begin(0)
    begin(1)

    def y_copy(stage, j, src, dst):
        return remote(src, dst, y_s.at[stage, j], y_r.at[stage, j], (me, others[j]))

    part_copies = [y_copy(0, j, psend.at[j], precv.at[j]) for j in range(peers - 1)]
    for j in range(peers - 1):

        @pl.loop(0, half // TILE)
        def _(t):
            src = pl.ds(pl.multiple_of(starts[j] + t * TILE, TILE), TILE)
            dst = pl.ds(pl.multiple_of(t * TILE, TILE), TILE)
            psend[j, :, dst] = jnp.dot(
                normed[...], wout[:, src], preferred_element_type=jnp.float32
            ).astype(jnp.bfloat16)

        part_copies[j].start()
    ring_step(0, 1)

    @pl.loop(0, half // TILE)
    def _(t):
        src = pl.ds(pl.multiple_of(mine + t * TILE, TILE), TILE)
        dst = pl.ds(pl.multiple_of(t * TILE, TILE), TILE)
        own[:, dst] = res[:, dst].astype(jnp.float32) + jnp.dot(
            normed[...], wout[:, src], preferred_element_type=jnp.float32
        )

    for k in range(2, ring):
        ring_step(0, k)
    begin(2)
    for copy in part_copies:
        copy.wait_recv()

    @pl.loop(0, half // TILE)
    def _(t):
        src = pl.ds(pl.multiple_of(t * TILE, TILE), TILE)
        dst = pl.ds(pl.multiple_of(mine + t * TILE, TILE), TILE)
        total = own[:, src]
        for j in range(peers - 1):
            total += precv[j, :, src].astype(jnp.float32)
        hid[:, dst] = total.astype(jnp.bfloat16)

    kept = hid.at[:, pl.ds(mine, half)]
    hid_copies = [y_copy(1, j, kept, kept) for j in range(peers - 1)]
    for copy in hid_copies:
        copy.start()
    x_steps(0)
    ring_steps(1)
    begin(3)
    for j in range(peers - 1):
        sender = lax.rem(y + peers - 1 - j, peers)
        place = hid.at[:, pl.ds(pl.multiple_of(sender * half, half), half)]
        y_copy(1, j, place, place).wait_recv()

    @pl.loop(0, toks // 64)
    def _(t):
        part = pl.ds(pl.multiple_of(t * 64, 64), 64)
        wide = hid[part, :].astype(jnp.float32)
        scale = lax.rsqrt(jnp.mean(wide * wide, axis=1, keepdims=True) + EPS)
        scaled[part, :] = (wide * scale * gain[...]).astype(jnp.bfloat16)

    x_steps(1)
    ring_step(2, 1)
    finish(0)
    finish(1)
    for k in range(2, ring):
        ring_step(2, k)
    ring_step(3, 1)

    @pl.loop(0, wg.shape[1] // TILE)
    def _(t):
        cols = pl.ds(pl.multiple_of(t * TILE, TILE), TILE)
        gate = jnp.dot(scaled[...], wg[:, cols], preferred_element_type=jnp.float32)
        up = jnp.dot(scaled[...], wu[:, cols], preferred_element_type=jnp.float32)
        act[:, cols] = (jax.nn.silu(gate) * up).astype(jnp.bfloat16)

    down_copies = [y_copy(2, j, dsend.at[j], drecv.at[j]) for j in range(peers - 1)]
    for j in range(peers - 1):
        p = 2 + j
        x_steps(p)
        for k in range(2, ring):
            ring_step(p + 1, k)
        if p + 2 < parts:
            begin(p + 2)
            ring_step(p + 2, 1)
        finish(p)

        @pl.loop(0, half // TILE)
        def _(t):
            cols = pl.ds(pl.multiple_of(t * TILE, TILE), TILE)
            dsend[j, :, cols] = jnp.dot(
                act[...], wd[j, :, cols], preferred_element_type=jnp.float32
            ).astype(jnp.bfloat16)

        down_copies[j].start()
    x_steps(parts - 1)
    finish(parts - 1)

    @pl.loop(0, half // TILE)
    def _(t):
        cols = pl.ds(pl.multiple_of(t * TILE, TILE), TILE)
        kept = pl.ds(pl.multiple_of(mine + t * TILE, TILE), TILE)
        own[:, cols] = hid[:, kept].astype(jnp.float32) + jnp.dot(
            act[...], wd[peers - 1, :, cols], preferred_element_type=jnp.float32
        )

    for copy in down_copies:
        copy.wait_recv()

    @pl.loop(0, half // TILE)
    def _(t):
        cols = pl.ds(pl.multiple_of(t * TILE, TILE), TILE)
        total = own[:, cols]
        for j in range(peers - 1):
            total += drecv[j, :, cols].astype(jnp.float32)
        out[:, cols] = (live[...] * total).astype(jnp.bfloat16)

    for copy in part_copies + hid_copies + down_copies:
        copy.wait_send()
    for p in range(parts):
        for k in range(ring):
            if k < ring - 1:
                ring_copy(p, k).wait_send()
            x_copy(p, k).wait_send()
        for k in range(2 * ring):
            sib_copy(p, k).wait_send()


def block(normed, residual, wout, gate_weight, up_weight, down_weight, mlp_gain, live):
    n, peers = lax.axis_size("ctx"), lax.axis_size("head")
    ring, parts = n // 4, 2 + peers
    toks, half = residual.shape
    width = wout.shape[1]
    deep = gate_weight.shape[0] * n
    units = gate_weight.shape[1]
    bf, f32 = jnp.bfloat16, jnp.float32
    sems = pltpu.SemaphoreType.DMA
    return pl.pallas_call(
        functools.partial(block_kernel, n, peers),
        out_shape=jax.ShapeDtypeStruct((toks, half), bf),
        in_specs=[pl.BlockSpec(memory_space=pltpu.VMEM)] * 8,
        out_specs=pl.BlockSpec(memory_space=pltpu.VMEM),
        scratch_shapes=[
            pltpu.VMEM((deep, units), bf),
            pltpu.VMEM((deep, units), bf),
            pltpu.VMEM((peers, units, half), bf),
            pltpu.VMEM((peers - 1, toks, half), bf),
            pltpu.VMEM((peers - 1, toks, half), bf),
            pltpu.VMEM((toks, half), f32),
            pltpu.VMEM((toks, width), bf),
            pltpu.VMEM((toks, width), bf),
            pltpu.VMEM((toks, units), bf),
            pltpu.VMEM((peers - 1, toks, half), bf),
            pltpu.VMEM((peers - 1, toks, half), bf),
            sems((parts, ring)), sems((parts, ring)),
            sems((parts, ring)), sems((parts, ring)),
            sems((parts, 2 * ring)), sems((parts, 2 * ring)),
            sems((3, peers - 1)), sems((3, peers - 1)),
        ],
        compiler_params=pltpu.CompilerParams(
            collective_id=0, has_side_effects=True, vmem_limit_bytes=60 * 1024 * 1024
        ),
        cost_estimate=pl.CostEstimate(
            flops=2 * toks * (2048 * width + 3 * deep * units),
            bytes_accessed=40 * 1024 * 1024,
            transcendentals=toks * units,
        ),
    )(normed, residual, wout, gate_weight, up_weight, down_weight, mlp_gain, live)


def shards(
    mixer_input,
    gate_input,
    write_vecs,
    read_vecs,
    log_decay,
    doc_start,
    live_mask,
    skip_gain,
    norm_gain,
    residual,
    out_weight,
    mlp_gain,
    gate_weight,
    up_weight,
    down_weight,
):
    tok_rows = mixer_input.shape[0]
    group_total = tok_rows // GROUP
    head_count = log_decay.shape[0]
    wout = lax.all_gather(out_weight, "ctx", axis=0, tiled=True)
    masked = mixer_input * live_mask.astype(jnp.bfloat16)[:, None]
    read_groups = read_vecs.reshape(group_total, GROUP, -1)
    group_data = (
        masked.reshape(group_total, GROUP, -1),
        write_vecs.reshape(group_total, GROUP, -1),
        read_groups,
        log_decay.reshape(head_count, group_total, GROUP).transpose(1, 0, 2),
        doc_start.reshape(group_total, GROUP),
    )

    def group_step(pieces):
        return group_core(pieces[0], pieces[1], pieces[2], pieces[3], pieces[4], skip_gain)

    directs, local_parts, reaches, decays = lax.map(group_step, group_data)
    run_state = jnp.zeros((head_count, HDIM, STATE), jnp.float32)
    run_factor = jnp.ones((head_count,), jnp.float32)
    before = []
    factors = []
    for group_id in range(group_total):
        before.append(run_state)
        factors.append(run_factor)
        run_state = decays[group_id][:, None, None] * run_state + local_parts[group_id]
        run_factor = run_factor * decays[group_id]
    incoming = carried_in(run_factor, run_state)
    outputs = []
    for group_id in range(group_total):
        inner_state = (factors[group_id][:, None, None] * incoming + before[group_id]).astype(
            jnp.bfloat16
        )
        crossed = jnp.einsum(
            "in,hpn->ihp", read_groups[group_id], inner_state, preferred_element_type=jnp.float32
        )
        outputs.append(directs[group_id] + crossed * reaches[group_id].T[:, :, None])
    output = jnp.concatenate(outputs, axis=0).reshape(tok_rows, -1)
    gated = output * jax.nn.silu(gate_input.astype(jnp.float32))
    squares = lax.psum(jnp.sum(gated * gated, axis=1), "head")
    normed = (gated * lax.rsqrt(squares / INNER + EPS)[:, None] * norm_gain).astype(jnp.bfloat16)
    return block(
        normed,
        residual,
        wout,
        gate_weight,
        up_weight,
        down_weight,
        mlp_gain[None, :],
        live_mask.astype(jnp.float32)[:, None],
    )


def solution(mesh):
    return jax.shard_map(
        shards,
        mesh=mesh,
        in_specs=(
            P("ctx", "head"),
            P("ctx", "head"),
            P("ctx", None),
            P("ctx", None),
            P("head", "ctx"),
            P("ctx"),
            P("ctx"),
            P("head"),
            P("head"),
            P("ctx", "head"),
            P(("head", "ctx"), None),
            P(),
            P("ctx", "head"),
            P("ctx", "head"),
            P(("head", "ctx"), None),
        ),
        out_specs=P("ctx", "head"),
        check_vma=False,
    )
```

```python
import functools

import jax
import jax.numpy as jnp
from jax import lax
from jax.experimental import pallas as pl
from jax.experimental.pallas import tpu as pltpu
from jax.sharding import PartitionSpec as P

HDIM = 64
STATE = 128
GROUP = 256
INNER = 4096
TILE = 256
LANES = 128

EPS = 1e-05
MESH = pl.DeviceIdType.MESH


def carried_in(factor, state):
    n = lax.axis_size("ctx")
    place = lax.axis_index("ctx")
    heads = state.shape[0]
    rows = heads * HDIM // n
    blocks = state.astype(jnp.bfloat16).reshape(n, rows, STATE)
    coarse = factor.astype(jnp.bfloat16)
    fine = (factor - coarse.astype(jnp.float32)).astype(jnp.bfloat16)
    tail = jnp.pad(jnp.stack([coarse, fine]), ((0, 14), (0, LANES - heads)))
    packed = jnp.concatenate([blocks, jnp.broadcast_to(tail[None], (n, 16, LANES))], axis=1)
    packed = lax.all_to_all(packed, "ctx", 0, 0)
    factors = packed[:, rows, :heads].astype(jnp.float32) + packed[:, rows + 1, :heads].astype(
        jnp.float32
    )
    owner = (place * rows + jnp.arange(rows)) // HDIM
    row_factors = jnp.take(factors, owner, axis=1)
    run = jnp.zeros((rows, STATE), jnp.float32)
    entering = []
    for source in range(n):
        entering.append(run.astype(jnp.bfloat16))
        run = row_factors[source][:, None] * run + packed[source, :rows].astype(jnp.float32)
    back = lax.all_to_all(jnp.stack(entering), "ctx", 0, 0)
    return back.reshape(heads, HDIM, STATE).astype(jnp.float32)


def group_core(masked, write_group, read_group, log_group, start_group, skip_gain):
    positions = jnp.arange(GROUP)
    log_sums = jnp.cumsum(log_group, axis=1)
    doc_index = jnp.cumsum(start_group)
    same_doc = (doc_index[:, None] == doc_index[None, :]) & (
        positions[:, None] >= positions[None, :]
    )
    scores = jnp.dot(read_group, write_group.T, preferred_element_type=jnp.float32)
    log_gaps = jnp.where(same_doc[None], log_sums[:, :, None] - log_sums[:, None, :], 0.0)
    weights = jnp.where(same_doc[None], scores[None] * jnp.exp(log_gaps), 0.0).astype(jnp.bfloat16)
    per_head = masked.reshape(GROUP, -1, HDIM)
    intra_out = jnp.einsum("hij,jhp->ihp", weights, per_head, preferred_element_type=jnp.float32)
    tail_wts = (
        jnp.exp(log_sums[:, -1:] - log_sums)
        * (doc_index == doc_index[-1]).astype(jnp.float32)[None]
    )
    weighted = (write_group.astype(jnp.float32)[None] * tail_wts[:, :, None]).astype(jnp.bfloat16)
    local_state = jnp.einsum("hjn,jhp->hpn", weighted, per_head, preferred_element_type=jnp.float32)
    reach_wts = jnp.exp(log_sums) * (doc_index == 0).astype(jnp.float32)[None]
    decay_all = jnp.exp(log_sums[:, -1]) * (doc_index[-1] == 0).astype(jnp.float32)
    direct = intra_out + skip_gain[None, :, None] * per_head.astype(jnp.float32)
    return (direct, local_state, reach_wts, decay_all)


def block_kernel(
    n, peers, normed, res, wout, wga, g_sh, u_sh, d_sh, gain, live, out,
    wg, wu, wd, psend, precv, own, hid, scaled, act, dsend, drecv,
    ring_s, ring_r, x_s, x_r, sib_s, sib_r, y_s, y_r,
):
    me, y = lax.axis_index("ctx"), lax.axis_index("head")
    c, b, a = me % 2, (me // 2) % 2, me // 4
    ring = n // 4
    half = res.shape[1]
    toks = res.shape[0]
    sib = (me + 1 - 2 * c, y)
    across = (me + 2 - 4 * b, y)
    after = (((a + 1) % ring) * 4 + b * 2 + c, y)
    before = (((a + ring - 1) % ring) * 4 + b * 2 + c, y)
    others = [lax.rem(y + j, peers) for j in range(1, peers)]
    mine = pl.multiple_of(y * half, half)
    starts = [pl.multiple_of(other * half, half) for other in others] + [mine]

    barrier = pltpu.get_barrier_semaphore()
    for device in [sib, across, after, before] + [(me, other) for other in others]:
        pl.semaphore_signal(barrier, inc=1, device_id=device, device_id_type=MESH)
    pl.semaphore_wait(barrier, 3 + peers)

    cut = wga.shape[1]
    full = [wg, wu] + [wd.at[j] for j in range(peers)]
    shard = [g_sh.at[:, pl.ds(cut, cut)], u_sh] + [d_sh.at[:, pl.ds(start, half)] for start in starts]
    parts = len(full)
    swap_first = (2,)

    def rows(p, k, bb, cc):
        slot = ((a + ring - k) % ring) * 4 + bb * 2 + cc
        depth = shard[p].shape[0]
        return pl.ds(pl.multiple_of(slot * depth, depth), depth)

    def remote(src, dst, send, recv, device):
        return pltpu.make_async_remote_copy(
            src_ref=src, dst_ref=dst, send_sem=send, recv_sem=recv,
            device_id=device, device_id_type=MESH,
        )

    def column(p, k):
        place = full[p].at[rows(p, k, b, c)]
        return (shard[p] if k == 0 else place), place

    def sib_chunk(p, k):
        if k < ring:
            return column(p, k)
        place = full[p].at[rows(p, k - ring, 1 - b, c)]
        return place, place

    def ring_copy(p, k):
        src, dst = sib_chunk(p, k)
        return remote(src, dst, ring_s.at[p, k], ring_r.at[p, k], after)

    def x_copy(p, k):
        src, dst = column(p, k)
        return remote(src, dst, x_s.at[p, k], x_r.at[p, k], across)

    def sib_copy(p, k):
        src, dst = sib_chunk(p, k)
        return remote(src, dst, sib_s.at[p, k], sib_r.at[p, k], sib)

    def swaps(p, k):
        return p not in swap_first or k == 0

    def spread(p, k):
        if k % ring < ring - 1:
            ring_copy(p, k).start()
        if k < ring and swaps(p, k):
            x_copy(p, k).start()
        sib_copy(p, k).start()

    def begin(p):
        spread(p, 0)
        full[p][rows(p, 0, b, c), :] = shard[p][...]

    def x_wait(p, k):
        place = full[p].at[rows(p, k, 1 - b, c)]
        remote(place, place, x_s.at[p, k], x_r.at[p, k], across).wait_recv()

    def swap(p):
        x_wait(p, 0)
        spread(p, ring)

    def ring_step(p, k):
        for lane in (k, ring + k) if p in swap_first else (k,):
            place = sib_chunk(p, lane)[1]
            remote(
                place, place, ring_s.at[p, lane - 1], ring_r.at[p, lane - 1], after
            ).wait_recv()
            spread(p, lane)

    def x_steps(p):
        if p not in swap_first:
            for k in range(ring):
                x_wait(p, k)
                sib_copy(p, ring + k).start()

    def finish(p):
        for k in range(2 * ring):
            bb = b if k < ring else 1 - b
            place = full[p].at[rows(p, k % ring, bb, 1 - c)]
            remote(place, place, sib_s.at[p, k], sib_r.at[p, k], sib).wait_recv()

    begin(0)
    begin(1)

    def y_copy(stage, j, src, dst):
        return remote(src, dst, y_s.at[stage, j], y_r.at[stage, j], (me, others[j]))

    part_copies = [y_copy(0, j, psend.at[j], precv.at[j]) for j in range(peers - 1)]
    for j in range(peers - 1):

        @pl.loop(0, half // TILE)
        def _(t):
            src = pl.ds(pl.multiple_of(starts[j] + t * TILE, TILE), TILE)
            dst = pl.ds(pl.multiple_of(t * TILE, TILE), TILE)
            psend[j, :, dst] = jnp.dot(
                normed[...], wout[:, src], preferred_element_type=jnp.float32
            ).astype(jnp.bfloat16)

        part_copies[j].start()
    ring_step(0, 1)
    begin(2)

    @pl.loop(0, half // TILE)
    def _(t):
        src = pl.ds(pl.multiple_of(mine + t * TILE, TILE), TILE)
        dst = pl.ds(pl.multiple_of(t * TILE, TILE), TILE)
        own[:, dst] = res[:, dst].astype(jnp.float32) + jnp.dot(
            normed[...], wout[:, src], preferred_element_type=jnp.float32
        )

    ring_step(1, 1)
    swap(2)
    for k in range(2, ring - 1):
        ring_step(0, k)
    for copy in part_copies:
        copy.wait_recv()

    @pl.loop(0, half // TILE)
    def _(t):
        src = pl.ds(pl.multiple_of(t * TILE, TILE), TILE)
        dst = pl.ds(pl.multiple_of(mine + t * TILE, TILE), TILE)
        total = own[:, src]
        for j in range(peers - 1):
            total += precv[j, :, src].astype(jnp.float32)
        hid[:, dst] = total.astype(jnp.bfloat16)

    kept = hid.at[:, pl.ds(mine, half)]
    hid_copies = [y_copy(1, j, kept, kept) for j in range(peers - 1)]
    for copy in hid_copies:
        copy.start()
    for k in range(2, ring - 1):
        ring_step(1, k)
    begin(3)
    ring_step(0, ring - 1)
    ring_step(1, ring - 1)
    ring_step(2, 1)
    ring_step(3, 1)
    x_steps(0)
    for j in range(peers - 1):
        sender = lax.rem(y + peers - 1 - j, peers)
        place = hid.at[:, pl.ds(pl.multiple_of(sender * half, half), half)]
        y_copy(1, j, place, place).wait_recv()

    @pl.loop(0, toks // 64)
    def _(t):
        part = pl.ds(pl.multiple_of(t * 64, 64), 64)
        wide = hid[part, :].astype(jnp.float32)
        scale = lax.rsqrt(jnp.mean(wide * wide, axis=1, keepdims=True) + EPS)
        scaled[part, :] = (wide * scale * gain[...]).astype(jnp.bfloat16)

    x_steps(1)
    for k in range(2, ring - 1):
        ring_step(2, k)
        ring_step(3, k)
    finish(0)
    finish(1)

    def gated_units(gate_ref, start):
        @pl.loop(0, cut // TILE)
        def _(t):
            cols = pl.ds(pl.multiple_of(t * TILE, TILE), TILE)
            wide = pl.ds(pl.multiple_of(start + t * TILE, TILE), TILE)
            gate = jnp.dot(scaled[...], gate_ref[:, cols], preferred_element_type=jnp.float32)
            up = jnp.dot(scaled[...], wu[:, wide], preferred_element_type=jnp.float32)
            act[:, wide] = (jax.nn.silu(gate) * up).astype(jnp.bfloat16)

    gated_units(wga, 0)
    ring_step(2, ring - 1)
    ring_step(3, ring - 1)
    x_steps(2)
    gated_units(wg, cut)

    down_copies = [y_copy(2, j, dsend.at[j], drecv.at[j]) for j in range(peers - 1)]
    for j in range(peers - 1):
        p = 2 + j
        if p + 2 < parts:
            begin(p + 2)
        if j > 0:
            x_steps(p)
        finish(p)

        @pl.loop(0, half // TILE)
        def _(t):
            cols = pl.ds(pl.multiple_of(t * TILE, TILE), TILE)
            dsend[j, :, cols] = jnp.dot(
                act[...], wd[j, :, cols], preferred_element_type=jnp.float32
            ).astype(jnp.bfloat16)

        down_copies[j].start()
        if p + 2 < parts:
            for k in range(1, ring):
                ring_step(p + 2, k)
    x_steps(parts - 1)
    finish(parts - 1)

    @pl.loop(0, half // TILE)
    def _(t):
        cols = pl.ds(pl.multiple_of(t * TILE, TILE), TILE)
        kept = pl.ds(pl.multiple_of(mine + t * TILE, TILE), TILE)
        own[:, cols] = hid[:, kept].astype(jnp.float32) + jnp.dot(
            act[...], wd[peers - 1, :, cols], preferred_element_type=jnp.float32
        )

    for copy in down_copies:
        copy.wait_recv()

    @pl.loop(0, half // TILE)
    def _(t):
        cols = pl.ds(pl.multiple_of(t * TILE, TILE), TILE)
        total = own[:, cols]
        for j in range(peers - 1):
            total += drecv[j, :, cols].astype(jnp.float32)
        out[:, cols] = (live[...] * total).astype(jnp.bfloat16)

    for copy in part_copies + hid_copies + down_copies:
        copy.wait_send()
    for p in range(parts):
        for k in range(2 * ring):
            sib_copy(p, k).wait_send()
            if k % ring < ring - 1 and (k < ring or p in swap_first):
                ring_copy(p, k).wait_send()
            if k < ring and swaps(p, k):
                x_copy(p, k).wait_send()


def block(normed, residual, wout, wga, gate_weight, up_weight, down_weight, mlp_gain, live):
    n, peers = lax.axis_size("ctx"), lax.axis_size("head")
    ring, parts = n // 4, 2 + peers
    toks, half = residual.shape
    width = wout.shape[1]
    deep = gate_weight.shape[0] * n
    units = gate_weight.shape[1]
    bf, f32 = jnp.bfloat16, jnp.float32
    sems = pltpu.SemaphoreType.DMA
    return pl.pallas_call(
        functools.partial(block_kernel, n, peers),
        out_shape=jax.ShapeDtypeStruct((toks, half), bf),
        in_specs=[pl.BlockSpec(memory_space=pltpu.VMEM)] * 9,
        out_specs=pl.BlockSpec(memory_space=pltpu.VMEM),
        scratch_shapes=[
            pltpu.VMEM((deep, units // 2), bf),
            pltpu.VMEM((deep, units), bf),
            pltpu.VMEM((peers, units, half), bf),
            pltpu.VMEM((peers - 1, toks, half), bf),
            pltpu.VMEM((peers - 1, toks, half), bf),
            pltpu.VMEM((toks, half), f32),
            pltpu.VMEM((toks, width), bf),
            pltpu.VMEM((toks, width), bf),
            pltpu.VMEM((toks, units), bf),
            pltpu.VMEM((peers - 1, toks, half), bf),
            pltpu.VMEM((peers - 1, toks, half), bf),
            sems((parts, 2 * ring)), sems((parts, 2 * ring)),
            sems((parts, ring)), sems((parts, ring)),
            sems((parts, 2 * ring)), sems((parts, 2 * ring)),
            sems((3, peers - 1)), sems((3, peers - 1)),
        ],
        compiler_params=pltpu.CompilerParams(
            collective_id=0, has_side_effects=True, vmem_limit_bytes=60 * 1024 * 1024
        ),
        cost_estimate=pl.CostEstimate(
            flops=2 * toks * (2048 * width + 3 * deep * units),
            bytes_accessed=40 * 1024 * 1024,
            transcendentals=toks * units,
        ),
    )(normed, residual, wout, wga, gate_weight, up_weight, down_weight, mlp_gain, live)


def shards(
    mixer_input,
    gate_input,
    write_vecs,
    read_vecs,
    log_decay,
    doc_start,
    live_mask,
    skip_gain,
    norm_gain,
    residual,
    out_weight,
    mlp_gain,
    gate_weight,
    up_weight,
    down_weight,
):
    tok_rows = mixer_input.shape[0]
    group_total = tok_rows // GROUP
    head_count = log_decay.shape[0]
    wout = lax.all_gather(out_weight, "ctx", axis=0, tiled=True)
    cut = gate_weight.shape[1] // 2
    wga = lax.all_gather(gate_weight[:, :cut], "ctx", axis=0, tiled=True)
    masked = mixer_input * live_mask.astype(jnp.bfloat16)[:, None]
    read_groups = read_vecs.reshape(group_total, GROUP, -1)
    group_data = (
        masked.reshape(group_total, GROUP, -1),
        write_vecs.reshape(group_total, GROUP, -1),
        read_groups,
        log_decay.reshape(head_count, group_total, GROUP).transpose(1, 0, 2),
        doc_start.reshape(group_total, GROUP),
    )

    def group_step(pieces):
        return group_core(pieces[0], pieces[1], pieces[2], pieces[3], pieces[4], skip_gain)

    directs, local_parts, reaches, decays = lax.map(group_step, group_data)
    run_state = jnp.zeros((head_count, HDIM, STATE), jnp.float32)
    run_factor = jnp.ones((head_count,), jnp.float32)
    before = []
    factors = []
    for group_id in range(group_total):
        before.append(run_state)
        factors.append(run_factor)
        run_state = decays[group_id][:, None, None] * run_state + local_parts[group_id]
        run_factor = run_factor * decays[group_id]
    incoming = carried_in(run_factor, run_state)
    outputs = []
    for group_id in range(group_total):
        inner_state = (factors[group_id][:, None, None] * incoming + before[group_id]).astype(
            jnp.bfloat16
        )
        crossed = jnp.einsum(
            "in,hpn->ihp", read_groups[group_id], inner_state, preferred_element_type=jnp.float32
        )
        outputs.append(directs[group_id] + crossed * reaches[group_id].T[:, :, None])
    output = jnp.concatenate(outputs, axis=0).reshape(tok_rows, -1)
    gated = output * jax.nn.silu(gate_input.astype(jnp.float32))
    squares = lax.psum(jnp.sum(gated * gated, axis=1), "head")
    normed = (gated * lax.rsqrt(squares / INNER + EPS)[:, None] * norm_gain).astype(jnp.bfloat16)
    return block(
        normed,
        residual,
        wout,
        wga,
        gate_weight,
        up_weight,
        down_weight,
        mlp_gain[None, :],
        live_mask.astype(jnp.float32)[:, None],
    )


def solution(mesh):
    return jax.shard_map(
        shards,
        mesh=mesh,
        in_specs=(
            P("ctx", "head"),
            P("ctx", "head"),
            P("ctx", None),
            P("ctx", None),
            P("head", "ctx"),
            P("ctx"),
            P("ctx"),
            P("head"),
            P("head"),
            P("ctx", "head"),
            P(("head", "ctx"), None),
            P(),
            P("ctx", "head"),
            P("ctx", "head"),
            P(("head", "ctx"), None),
        ),
        out_specs=P("ctx", "head"),
        check_vma=False,
    )
```

```python
import functools

import jax
import jax.numpy as jnp
from jax import lax
from jax.experimental import pallas as pl
from jax.experimental.pallas import tpu as pltpu
from jax.sharding import PartitionSpec as P

HDIM = 64
STATE = 128
GROUP = 256
INNER = 4096
TILE = 256
LANES = 128

EPS = 1e-05
MESH = pl.DeviceIdType.MESH


def carried_in(factor, state):
    n = lax.axis_size("ctx")
    place = lax.axis_index("ctx")
    heads = state.shape[0]
    rows = heads * HDIM // n
    blocks = state.astype(jnp.bfloat16).reshape(n, rows, STATE)
    coarse = factor.astype(jnp.bfloat16)
    fine = (factor - coarse.astype(jnp.float32)).astype(jnp.bfloat16)
    tail = jnp.pad(jnp.stack([coarse, fine]), ((0, 14), (0, LANES - heads)))
    packed = jnp.concatenate([blocks, jnp.broadcast_to(tail[None], (n, 16, LANES))], axis=1)
    packed = lax.all_to_all(packed, "ctx", 0, 0)
    factors = packed[:, rows, :heads].astype(jnp.float32) + packed[:, rows + 1, :heads].astype(
        jnp.float32
    )
    owner = (place * rows + jnp.arange(rows)) // HDIM
    row_factors = jnp.take(factors, owner, axis=1)
    run = jnp.zeros((rows, STATE), jnp.float32)
    entering = []
    for source in range(n):
        entering.append(run.astype(jnp.bfloat16))
        run = row_factors[source][:, None] * run + packed[source, :rows].astype(jnp.float32)
    back = lax.all_to_all(jnp.stack(entering), "ctx", 0, 0)
    return back.reshape(heads, HDIM, STATE).astype(jnp.float32)


def group_core(masked, write_group, read_group, log_group, start_group, skip_gain):
    positions = jnp.arange(GROUP)
    log_sums = jnp.cumsum(log_group, axis=1)
    doc_index = jnp.cumsum(start_group)
    same_doc = (doc_index[:, None] == doc_index[None, :]) & (
        positions[:, None] >= positions[None, :]
    )
    scores = jnp.dot(read_group, write_group.T, preferred_element_type=jnp.float32)
    log_gaps = jnp.where(same_doc[None], log_sums[:, :, None] - log_sums[:, None, :], 0.0)
    weights = jnp.where(same_doc[None], scores[None] * jnp.exp(log_gaps), 0.0).astype(jnp.bfloat16)
    per_head = masked.reshape(GROUP, -1, HDIM)
    intra_out = jnp.einsum("hij,jhp->ihp", weights, per_head, preferred_element_type=jnp.float32)
    tail_wts = (
        jnp.exp(log_sums[:, -1:] - log_sums)
        * (doc_index == doc_index[-1]).astype(jnp.float32)[None]
    )
    weighted = (write_group.astype(jnp.float32)[None] * tail_wts[:, :, None]).astype(jnp.bfloat16)
    local_state = jnp.einsum("hjn,jhp->hpn", weighted, per_head, preferred_element_type=jnp.float32)
    reach_wts = jnp.exp(log_sums) * (doc_index == 0).astype(jnp.float32)[None]
    decay_all = jnp.exp(log_sums[:, -1]) * (doc_index[-1] == 0).astype(jnp.float32)
    direct = intra_out + skip_gain[None, :, None] * per_head.astype(jnp.float32)
    return (direct, local_state, reach_wts, decay_all)


def block_kernel(
    n, peers, normed, res, both, g_sh, u_sh, d_sh, gain, live, out,
    wg, wu, wd, psend, precv, own, hid, scaled, act, dsend, drecv,
    ring_s, ring_r, x_s, x_r, sib_s, sib_r, y_s, y_r,
):
    me, y = lax.axis_index("ctx"), lax.axis_index("head")
    c, b, a = me % 2, (me // 2) % 2, me // 4
    ring = n // 4
    half = res.shape[1]
    toks = res.shape[0]
    sib = (me + 1 - 2 * c, y)
    across = (me + 2 - 4 * b, y)
    after = (((a + 1) % ring) * 4 + b * 2 + c, y)
    before = (((a + ring - 1) % ring) * 4 + b * 2 + c, y)
    others = [lax.rem(y + j, peers) for j in range(1, peers)]
    mine = pl.multiple_of(y * half, half)
    starts = [pl.multiple_of(other * half, half) for other in others] + [mine]

    barrier = pltpu.get_barrier_semaphore()
    for device in [sib, across, after, before] + [(me, other) for other in others]:
        pl.semaphore_signal(barrier, inc=1, device_id=device, device_id_type=MESH)
    pl.semaphore_wait(barrier, 3 + peers)

    width = hid.shape[1]
    cut = wg.shape[1]
    wout = both.at[pl.ds(0, normed.shape[1]), pl.ds(0, width)]
    wga = both.at[:, pl.ds(width, cut)]
    full = [wg, wu] + [wd.at[j] for j in range(peers)]
    shard = [g_sh.at[:, pl.ds(cut, cut)], u_sh] + [d_sh.at[:, pl.ds(start, half)] for start in starts]
    parts = len(full)
    swap_first = (2,)

    def rows(p, k, bb, cc):
        slot = ((a + ring - k) % ring) * 4 + bb * 2 + cc
        depth = shard[p].shape[0]
        return pl.ds(pl.multiple_of(slot * depth, depth), depth)

    def remote(src, dst, send, recv, device):
        return pltpu.make_async_remote_copy(
            src_ref=src, dst_ref=dst, send_sem=send, recv_sem=recv,
            device_id=device, device_id_type=MESH,
        )

    def column(p, k):
        place = full[p].at[rows(p, k, b, c)]
        return (shard[p] if k == 0 else place), place

    def sib_chunk(p, k):
        if k < ring:
            return column(p, k)
        place = full[p].at[rows(p, k - ring, 1 - b, c)]
        return place, place

    def ring_copy(p, k):
        src, dst = sib_chunk(p, k)
        return remote(src, dst, ring_s.at[p, k], ring_r.at[p, k], after)

    def x_copy(p, k):
        src, dst = column(p, k)
        return remote(src, dst, x_s.at[p, k], x_r.at[p, k], across)

    def sib_copy(p, k):
        src, dst = sib_chunk(p, k)
        return remote(src, dst, sib_s.at[p, k], sib_r.at[p, k], sib)

    def swaps(p, k):
        return p not in swap_first or k == 0

    def spread(p, k):
        if k % ring < ring - 1:
            ring_copy(p, k).start()
        if k < ring and swaps(p, k):
            x_copy(p, k).start()
        sib_copy(p, k).start()

    def begin(p):
        spread(p, 0)
        full[p][rows(p, 0, b, c), :] = shard[p][...]

    def x_wait(p, k):
        place = full[p].at[rows(p, k, 1 - b, c)]
        remote(place, place, x_s.at[p, k], x_r.at[p, k], across).wait_recv()

    def swap(p):
        x_wait(p, 0)
        spread(p, ring)

    def ring_step(p, k):
        for lane in (k, ring + k) if p in swap_first else (k,):
            place = sib_chunk(p, lane)[1]
            remote(
                place, place, ring_s.at[p, lane - 1], ring_r.at[p, lane - 1], after
            ).wait_recv()
            spread(p, lane)

    def x_steps(p):
        if p not in swap_first:
            for k in range(ring):
                x_wait(p, k)
                sib_copy(p, ring + k).start()

    def finish(p):
        for k in range(2 * ring):
            bb = b if k < ring else 1 - b
            place = full[p].at[rows(p, k % ring, bb, 1 - c)]
            remote(place, place, sib_s.at[p, k], sib_r.at[p, k], sib).wait_recv()

    begin(0)
    begin(1)

    def y_copy(stage, j, src, dst):
        return remote(src, dst, y_s.at[stage, j], y_r.at[stage, j], (me, others[j]))

    part_copies = [y_copy(0, j, psend.at[j], precv.at[j]) for j in range(peers - 1)]
    for j in range(peers - 1):

        @pl.loop(0, half // TILE)
        def _(t):
            src = pl.ds(pl.multiple_of(starts[j] + t * TILE, TILE), TILE)
            dst = pl.ds(pl.multiple_of(t * TILE, TILE), TILE)
            psend[j, :, dst] = jnp.dot(
                normed[...], wout[:, src], preferred_element_type=jnp.float32
            ).astype(jnp.bfloat16)

        part_copies[j].start()
    ring_step(0, 1)
    begin(2)

    @pl.loop(0, half // TILE)
    def _(t):
        src = pl.ds(pl.multiple_of(mine + t * TILE, TILE), TILE)
        dst = pl.ds(pl.multiple_of(t * TILE, TILE), TILE)
        own[:, dst] = res[:, dst].astype(jnp.float32) + jnp.dot(
            normed[...], wout[:, src], preferred_element_type=jnp.float32
        )

    ring_step(1, 1)
    swap(2)
    for k in range(2, ring - 1):
        ring_step(0, k)
    for copy in part_copies:
        copy.wait_recv()

    @pl.loop(0, half // TILE)
    def _(t):
        src = pl.ds(pl.multiple_of(t * TILE, TILE), TILE)
        dst = pl.ds(pl.multiple_of(mine + t * TILE, TILE), TILE)
        total = own[:, src]
        for j in range(peers - 1):
            total += precv[j, :, src].astype(jnp.float32)
        hid[:, dst] = total.astype(jnp.bfloat16)

    kept = hid.at[:, pl.ds(mine, half)]
    hid_copies = [y_copy(1, j, kept, kept) for j in range(peers - 1)]
    for copy in hid_copies:
        copy.start()
    for k in range(2, ring - 1):
        ring_step(1, k)
    begin(3)
    ring_step(0, ring - 1)
    ring_step(1, ring - 1)
    ring_step(2, 1)
    ring_step(3, 1)
    x_steps(0)
    for j in range(peers - 1):
        sender = lax.rem(y + peers - 1 - j, peers)
        place = hid.at[:, pl.ds(pl.multiple_of(sender * half, half), half)]
        y_copy(1, j, place, place).wait_recv()

    @pl.loop(0, toks // 64)
    def _(t):
        part = pl.ds(pl.multiple_of(t * 64, 64), 64)
        wide = hid[part, :].astype(jnp.float32)
        scale = lax.rsqrt(jnp.mean(wide * wide, axis=1, keepdims=True) + EPS)
        scaled[part, :] = (wide * scale * gain[...]).astype(jnp.bfloat16)

    x_steps(1)
    for k in range(2, ring - 1):
        ring_step(2, k)
        ring_step(3, k)
    finish(0)
    finish(1)

    def gated_units(gate_ref, start):
        @pl.loop(0, cut // TILE)
        def _(t):
            cols = pl.ds(pl.multiple_of(t * TILE, TILE), TILE)
            wide = pl.ds(pl.multiple_of(start + t * TILE, TILE), TILE)
            gate = jnp.dot(scaled[...], gate_ref[:, cols], preferred_element_type=jnp.float32)
            up = jnp.dot(scaled[...], wu[:, wide], preferred_element_type=jnp.float32)
            act[:, wide] = (jax.nn.silu(gate) * up).astype(jnp.bfloat16)

    gated_units(wga, 0)
    ring_step(2, ring - 1)
    ring_step(3, ring - 1)
    x_steps(2)
    gated_units(wg, cut)

    down_copies = [y_copy(2, j, dsend.at[j], drecv.at[j]) for j in range(peers - 1)]
    for j in range(peers - 1):
        p = 2 + j
        if p + 2 < parts:
            begin(p + 2)
        if j > 0:
            x_steps(p)
        finish(p)

        @pl.loop(0, half // TILE)
        def _(t):
            cols = pl.ds(pl.multiple_of(t * TILE, TILE), TILE)
            dsend[j, :, cols] = jnp.dot(
                act[...], wd[j, :, cols], preferred_element_type=jnp.float32
            ).astype(jnp.bfloat16)

        down_copies[j].start()
        if p + 2 < parts:
            for k in range(1, ring):
                ring_step(p + 2, k)
    x_steps(parts - 1)
    finish(parts - 1)

    @pl.loop(0, half // TILE)
    def _(t):
        cols = pl.ds(pl.multiple_of(t * TILE, TILE), TILE)
        kept = pl.ds(pl.multiple_of(mine + t * TILE, TILE), TILE)
        own[:, cols] = hid[:, kept].astype(jnp.float32) + jnp.dot(
            act[...], wd[peers - 1, :, cols], preferred_element_type=jnp.float32
        )

    for copy in down_copies:
        copy.wait_recv()

    @pl.loop(0, half // TILE)
    def _(t):
        cols = pl.ds(pl.multiple_of(t * TILE, TILE), TILE)
        total = own[:, cols]
        for j in range(peers - 1):
            total += drecv[j, :, cols].astype(jnp.float32)
        out[:, cols] = (live[...] * total).astype(jnp.bfloat16)

    for copy in part_copies + hid_copies + down_copies:
        copy.wait_send()
    for p in range(parts):
        for k in range(2 * ring):
            sib_copy(p, k).wait_send()
            if k % ring < ring - 1 and (k < ring or p in swap_first):
                ring_copy(p, k).wait_send()
            if k < ring and swaps(p, k):
                x_copy(p, k).wait_send()


def gather_both(out_rows, gate_rows):
    split = gate_rows.shape[0] // out_rows.shape[0]
    gates = gate_rows.reshape(out_rows.shape[0], -1)
    whole = lax.all_gather(jnp.concatenate([out_rows, gates], axis=1), "ctx", axis=0, tiled=True)
    if split == 1:
        return whole
    width = out_rows.shape[1]
    gates = whole[:, width:].reshape(whole.shape[0] * split, -1)
    outs = jnp.pad(whole[:, :width], ((0, gates.shape[0] - whole.shape[0]), (0, 0)))
    return jnp.concatenate([outs, gates], axis=1)


def block(normed, residual, both, gate_weight, up_weight, down_weight, mlp_gain, live):
    n, peers = lax.axis_size("ctx"), lax.axis_size("head")
    ring, parts = n // 4, 2 + peers
    toks, half = residual.shape
    width = half * peers
    deep = gate_weight.shape[0] * n
    units = gate_weight.shape[1]
    bf, f32 = jnp.bfloat16, jnp.float32
    sems = pltpu.SemaphoreType.DMA
    return pl.pallas_call(
        functools.partial(block_kernel, n, peers),
        out_shape=jax.ShapeDtypeStruct((toks, half), bf),
        in_specs=[pl.BlockSpec(memory_space=pltpu.VMEM)] * 8,
        out_specs=pl.BlockSpec(memory_space=pltpu.VMEM),
        scratch_shapes=[
            pltpu.VMEM((deep, units // 2), bf),
            pltpu.VMEM((deep, units), bf),
            pltpu.VMEM((peers, units, half), bf),
            pltpu.VMEM((peers - 1, toks, half), bf),
            pltpu.VMEM((peers - 1, toks, half), bf),
            pltpu.VMEM((toks, half), f32),
            pltpu.VMEM((toks, width), bf),
            pltpu.VMEM((toks, width), bf),
            pltpu.VMEM((toks, units), bf),
            pltpu.VMEM((peers - 1, toks, half), bf),
            pltpu.VMEM((peers - 1, toks, half), bf),
            sems((parts, 2 * ring)), sems((parts, 2 * ring)),
            sems((parts, ring)), sems((parts, ring)),
            sems((parts, 2 * ring)), sems((parts, 2 * ring)),
            sems((3, peers - 1)), sems((3, peers - 1)),
        ],
        compiler_params=pltpu.CompilerParams(
            collective_id=0, has_side_effects=True, vmem_limit_bytes=60 * 1024 * 1024
        ),
        cost_estimate=pl.CostEstimate(
            flops=2 * toks * (2048 * width + 3 * deep * units),
            bytes_accessed=40 * 1024 * 1024,
            transcendentals=toks * units,
        ),
    )(normed, residual, both, gate_weight, up_weight, down_weight, mlp_gain, live)


def shards(
    mixer_input,
    gate_input,
    write_vecs,
    read_vecs,
    log_decay,
    doc_start,
    live_mask,
    skip_gain,
    norm_gain,
    residual,
    out_weight,
    mlp_gain,
    gate_weight,
    up_weight,
    down_weight,
):
    tok_rows = mixer_input.shape[0]
    group_total = tok_rows // GROUP
    head_count = log_decay.shape[0]
    cut = gate_weight.shape[1] // 2
    both = gather_both(out_weight, gate_weight[:, :cut])
    masked = mixer_input * live_mask.astype(jnp.bfloat16)[:, None]
    read_groups = read_vecs.reshape(group_total, GROUP, -1)
    group_data = (
        masked.reshape(group_total, GROUP, -1),
        write_vecs.reshape(group_total, GROUP, -1),
        read_groups,
        log_decay.reshape(head_count, group_total, GROUP).transpose(1, 0, 2),
        doc_start.reshape(group_total, GROUP),
    )

    def group_step(pieces):
        return group_core(pieces[0], pieces[1], pieces[2], pieces[3], pieces[4], skip_gain)

    directs, local_parts, reaches, decays = lax.map(group_step, group_data)
    run_state = jnp.zeros((head_count, HDIM, STATE), jnp.float32)
    run_factor = jnp.ones((head_count,), jnp.float32)
    before = []
    factors = []
    for group_id in range(group_total):
        before.append(run_state)
        factors.append(run_factor)
        run_state = decays[group_id][:, None, None] * run_state + local_parts[group_id]
        run_factor = run_factor * decays[group_id]
    incoming = carried_in(run_factor, run_state)
    outputs = []
    for group_id in range(group_total):
        inner_state = (factors[group_id][:, None, None] * incoming + before[group_id]).astype(
            jnp.bfloat16
        )
        crossed = jnp.einsum(
            "in,hpn->ihp", read_groups[group_id], inner_state, preferred_element_type=jnp.float32
        )
        outputs.append(directs[group_id] + crossed * reaches[group_id].T[:, :, None])
    output = jnp.concatenate(outputs, axis=0).reshape(tok_rows, -1)
    gated = output * jax.nn.silu(gate_input.astype(jnp.float32))
    squares = lax.psum(jnp.sum(gated * gated, axis=1), "head")
    normed = (gated * lax.rsqrt(squares / INNER + EPS)[:, None] * norm_gain).astype(jnp.bfloat16)
    return block(
        normed,
        residual,
        both,
        gate_weight,
        up_weight,
        down_weight,
        mlp_gain[None, :],
        live_mask.astype(jnp.float32)[:, None],
    )


def solution(mesh):
    return jax.shard_map(
        shards,
        mesh=mesh,
        in_specs=(
            P("ctx", "head"),
            P("ctx", "head"),
            P("ctx", None),
            P("ctx", None),
            P("head", "ctx"),
            P("ctx"),
            P("ctx"),
            P("head"),
            P("head"),
            P("ctx", "head"),
            P(("head", "ctx"), None),
            P(),
            P("ctx", "head"),
            P("ctx", "head"),
            P(("head", "ctx"), None),
        ),
        out_specs=P("ctx", "head"),
        check_vma=False,
    )
```
